32 devices in a mesh: groups: 2 (over y), factor: 4 (over z), dp: 2 (over x), query: 2 (over core).
Axes of the slice: x: 2, y: 2, z: 4, core: 2. Of those that a mesh axis runs over, the one named last changes fastest.
Arguments:
- grad_factors: float32 [192, 14336], P(('groups', 'factor'), ('dp', 'query')), parts along dimension 0, may hold values from -6 to 6
- act_factors: float32 [192, 4096], P(('groups', 'dp', 'query'), 'factor'), parts along dimension 0, may hold values from -6 to 6
- seq_ids: int32 [192], P('groups'), parts along dimension 0, may hold values from 0 to 3, never falling along the last dimension, each value on 1 to 48 neighbouring positions
- out_basis: float32 [14336, 14336], P(('dp', 'query'), 'factor'), may hold values from -0.046875 to 0.046875
- in_basis: float32 [4096, 4096], P('factor', ('dp', 'query')), may hold values from -0.09375 to 0.09375
- eigenvalues: float32 [14336, 4096], P('factor', ('dp', 'query')), may hold values from 0.05 to 5
- damping: float32 [1], replicated, may hold values from 0.02 to 0.2
- query_out: float32 [256, 2, 14336], P(('dp', 'query'), None, 'factor'), may hold values from -0.005859375 to 0.005859375
- query_in: float32 [256, 2, 4096], P('factor', None, ('dp', 'query')), may hold values from -0.005859375 to 0.005859375
- query_ids: int32 [256], replicated, may hold values from 0 to 255, each once
Outputs:
- scores: float32 [8, 256], P('groups', ('factor', 'dp', 'query')), parts along dimension 0
The draws below stay inside these ranges and needn't reach their ends.
There are 2 independent parts, one for each index of `groups`. The reference program is written for one: setup_inputs(seed, part) draws one part's arguments, and reference() takes and returns one part's arrays. A program takes and returns all parts, laid end to end along the dimension named above; an argument that names none is the same for every part. Nothing has to cross between parts.
Inputs may be any that keep to these rules, and one draw needn't show every extreme that they name: `seq_ids`: ids never fall along the tokens, and every sequence holds at least one token. `query_ids`: each query appears once.
All inputs are finite; a program needn't handle non-finite values.
Results may differ from the reference program's by a relative error of at most 0.0003.
Values sent between devices are 32-bit elements; how exact they have to be, the bound alone decides.
A program may use at most 384 MiB of HBM per device.

```python
import math
import jax
import jax.numpy as jnp
import numpy as np
from jax import lax

D_OUT = 14336
D_IN = 4096
SEQS = 4
NQ = 256
QR = 2
TOKENS = 96


def block_levels(stream_key, dims, shards, low, largest):
    factor_of = 1.0
    for axis_at, blocks in shards:
        steps = jax.random.uniform(jax.random.fold_in(jax.random.fold_in(stream_key, 6), axis_at), (blocks,), jnp.float32, low / len(shards), largest / len(shards))
        factor_of = factor_of * jnp.repeat(jnp.exp(steps), dims[axis_at] // blocks).reshape((-1,) + (1,) * (len(dims) - 1 - axis_at))
    return factor_of


def profile(number_of, total, bound, skew):
    weights = [(1 << 20) // math.isqrt(standing ** skew) + 1 for standing in range(2, number_of + 1)]
    spare, given = total - bound - (number_of - 1), [1] * (number_of - 1)
    while spare > 0:
        candidates = [i for i in range(number_of - 1) if given[i] < bound]
        pool, left = sum([weights[i] for i in candidates]), spare
        for i in candidates:
            addition = min(bound - given[i], max(1, left * weights[i] // pool), spare)
            given[i] = given[i] + addition
            spare = spare - addition
    return np.array([bound] + given)


def uneven_parts(own_key, number_of, total, bound, lean):
    if number_of == 2:
        one = jax.random.randint(own_key, (), max(1, total - bound), min(bound, total - 1) + 1)
        return jnp.stack([one, total - one])
    tallies = jnp.asarray(profile(number_of, total, bound, lean), jnp.int32)
    couples = (number_of - 1) // 2
    giver, sink = tallies[1:1 + 2 * couples:2], tallies[2:2 + 2 * couples:2]
    margin = jnp.minimum(giver - 1, bound - sink)
    moved = jax.random.randint(jax.random.fold_in(own_key, 1), (couples,), 0, 1 << 20) % (margin + 1)
    tallies = tallies.at[1:1 + 2 * couples:2].set(giver - moved).at[2:2 + 2 * couples:2].set(sink + moved)
    return tallies[jax.random.permutation(jax.random.fold_in(own_key, 2), number_of)]


def normal_values(key, shape, scale, bound, split=(), held_as=jnp.bfloat16):
    values = jax.random.normal(key, shape, jnp.float32) * scale
    if len(split) > 0:
        values = block_levels(key, shape, split, -0.22, 0.18) * values
    return jnp.clip(values, min=-bound, max=bound).astype(held_as)


def setup_inputs(seed: int = 0, part: int = 0) -> dict:
    key_of = jax.random.split(jax.random.key(seed), 11)
    own_keys = jax.random.split(jax.random.fold_in(key_of[10], part), 11)
    grad_factors = normal_values(own_keys[0], (TOKENS, D_OUT), 1.0, 6.0, ((0, 4), (1, 4)), jnp.float32)
    act_factors = normal_values(own_keys[1], (TOKENS, D_IN), 1.0, 6.0, ((0, 4), (1, 4)), jnp.float32)
    seq_ids = jnp.searchsorted(jnp.cumsum(uneven_parts(own_keys[2], SEQS, TOKENS, TOKENS // 2, 2)), jnp.arange(TOKENS), side="right").astype(jnp.int32)
    out_basis = normal_values(key_of[3], (D_OUT, D_OUT), D_OUT ** -0.5, 0.046875, ((0, 4), (1, 4)), jnp.float32)
    in_basis = normal_values(key_of[4], (D_IN, D_IN), D_IN ** -0.5, 0.09375, ((0, 4), (1, 4)), jnp.float32)
    eigenvalues = jnp.clip(jnp.exp(math.log(5.0) - 4.6051702 * jax.random.uniform(key_of[5], (D_OUT, D_IN), jnp.float32) ** block_levels(key_of[5], (D_OUT, D_IN), ((0, 4), (1, 4)), -0.2, 0.2)), 0.05, 5.0)
    damping = jnp.clip(jnp.exp(jax.random.uniform(key_of[6], (1,), jnp.float32, math.log(0.02), math.log(0.2))), 0.02, 0.2)
    query_out = normal_values(key_of[7], (NQ, QR, D_OUT), (D_OUT * 64) ** -0.5, 0.005859375, ((0, 4), (2, 4)), jnp.float32)
    query_in = normal_values(key_of[8], (NQ, QR, D_IN), (D_IN * 256) ** -0.5, 0.005859375, ((0, 4), (2, 4)), jnp.float32)
    query_ids = jax.random.permutation(key_of[9], NQ).astype(jnp.int32)
    return {"grad_factors": grad_factors, "act_factors": act_factors, "seq_ids": seq_ids, "out_basis": out_basis, "in_basis": in_basis, "eigenvalues": eigenvalues, "damping": damping, "query_out": query_out, "query_in": query_in, "query_ids": query_ids}


def reference(grad_factors, act_factors, seq_ids, out_basis, in_basis, eigenvalues, damping, query_out, query_in, query_ids):
    highest = lax.Precision.HIGHEST
    rotated_grads = jnp.dot(grad_factors, out_basis, precision=highest, preferred_element_type=jnp.float32)
    rotated_acts = jnp.dot(act_factors, in_basis, precision=highest, preferred_element_type=jnp.float32)
    query_left = query_out.reshape(NQ * QR, D_OUT)
    query_right = query_in.reshape(NQ * QR, D_IN)
    shift = eigenvalues + damping[0]

    def one_sequence(index):
        member = (seq_ids == index).astype(jnp.float32)
        weighted = rotated_acts * member[:, None]
        grad_seq = lax.dot_general(rotated_grads, weighted, (((0,), (0,)), ((), ())), precision=highest, preferred_element_type=jnp.float32)
        precond = grad_seq / shift
        cross = lax.dot_general(precond, query_right, (((1,), (1,)), ((), ())), precision=highest, preferred_element_type=jnp.float32)
        totals = jnp.sum(cross * query_left.T, axis=0)
        return jnp.sum(totals.reshape(NQ, QR), axis=1)

    raw = lax.map(one_sequence, jnp.arange(SEQS, dtype=jnp.int32))
    return raw[:, query_ids]
```

```python
import functools

import jax
import jax.numpy as jnp
from jax import lax
from jax.experimental import pallas as pl
from jax.experimental.pallas import tpu as pltpu
from jax.sharding import PartitionSpec as P

SEQS = 4
F32 = jnp.float32
BF16 = jnp.bfloat16
VMEM_BYTES = 56 * 1024 * 1024


def tile_of(width, most):
    for tile in range(most, 0, -128):
        if width % tile == 0:
            return tile
    return width


def halves(x):
    high = x.astype(BF16)
    return high, (x - high.astype(F32)).astype(BF16)


def dot(a, b, contract=((1,), (0,))):
    return lax.dot_general(a, b, (contract, ((), ())), preferred_element_type=F32)


def rotate_kernel(x_ref, basis_ref, out_ref, x_both):
    rows = x_ref.shape[0]

    @pl.when(pl.program_id(0) == 0)
    def _():
        high, low = halves(x_ref[...])
        x_both[:rows, :] = high
        x_both[rows:, :] = low

    high, low = halves(basis_ref[...])
    both = dot(x_both[...], high)
    out_ref[...] = both[:rows] + both[rows:] + dot(x_both[:rows, :], low)


def rotate(x, basis, part, parts):
    rows, depth = x.shape
    width = basis.shape[1] // parts
    tile = tile_of(width, 512)
    steps = width // tile
    return pl.pallas_call(
        rotate_kernel,
        grid=(steps,),
        in_specs=[
            pl.BlockSpec((rows, depth), lambda n: (0, 0)),
            pl.BlockSpec((depth, tile), lambda n: (0, part * steps + n)),
        ],
        out_specs=pl.BlockSpec((rows, tile), lambda n: (0, n)),
        out_shape=jax.ShapeDtypeStruct((rows, width), F32),
        scratch_shapes=[pltpu.VMEM((2 * rows, depth), BF16)],
        compiler_params=pltpu.CompilerParams(vmem_limit_bytes=VMEM_BYTES),
        cost_estimate=pl.CostEstimate(
            flops=6 * rows * depth * width, bytes_accessed=4 * depth * width, transcendentals=0
        ),
        name="rotate",
    )(x, basis)


def score_kernel(ids_ref, damping_ref, acts_ref, grads_ref, eig_ref, right_ref, left_ref, out_ref, weighted, right_high, right_low):
    tokens, inner = acts_ref.shape

    @pl.when(pl.program_id(0) == 0)
    def _():
        out_ref[...] = jnp.zeros_like(out_ref)
        for s in range(SEQS):
            member = ids_ref[...] == s
            high, low = halves(jnp.where(member, acts_ref[...], 0.0))
            cols = slice(s * inner, (s + 1) * inner)
            weighted[:tokens, cols] = high
            weighted[tokens : 2 * tokens, cols] = low
            weighted[2 * tokens :, cols] = high
        high, low = halves(right_ref[...].T)
        right_high[...] = high
        right_low[...] = low

    rows = eig_ref.shape[0]
    inverse = 1.0 / (eig_ref[...] + damping_ref[0])
    grad_high, grad_low = halves(grads_ref[...])
    grad_all = jnp.concatenate([grad_high, grad_high, grad_low], axis=0)
    left = left_ref[...].T
    for s in range(SEQS):
        grad_seq = dot(grad_all, weighted[:, s * inner : (s + 1) * inner], ((0,), (0,)))
        high, low = halves(grad_seq * inverse)
        cross = dot(high, right_high[...]) + dot(high, right_low[...]) + dot(low, right_high[...])
        terms = (cross * left).reshape(rows // 8, 8, cross.shape[1])
        out_ref[s * 8 : (s + 1) * 8, :] += jnp.sum(terms, axis=0)


def score(ids, damping, acts, grads, eigenvalues, right, left, part, parts):
    tokens, inner = acts.shape
    queries = right.shape[0]
    outer = eigenvalues.shape[0] // parts
    tile = tile_of(outer, 256)
    steps = outer // tile
    whole = lambda i: (0, 0)
    return pl.pallas_call(
        score_kernel,
        grid=(steps,),
        in_specs=[
            pl.BlockSpec((tokens, 1), whole),
            pl.BlockSpec(memory_space=pltpu.SMEM),
            pl.BlockSpec((tokens, inner), whole),
            pl.BlockSpec((tokens, tile), lambda i: (0, i)),
            pl.BlockSpec((tile, inner), lambda i: (part * steps + i, 0)),
            pl.BlockSpec((queries, inner), whole),
            pl.BlockSpec((queries, tile), lambda i: (0, part * steps + i)),
        ],
        out_specs=pl.BlockSpec((SEQS * 8, queries), whole),
        out_shape=jax.ShapeDtypeStruct((SEQS * 8, queries), F32),
        scratch_shapes=[
            pltpu.VMEM((3 * tokens, SEQS * inner), BF16),
            pltpu.VMEM((inner, queries), BF16),
            pltpu.VMEM((inner, queries), BF16),
        ],
        compiler_params=pltpu.CompilerParams(vmem_limit_bytes=VMEM_BYTES),
        cost_estimate=pl.CostEstimate(
            flops=6 * SEQS * outer * inner * (queries + 2 * tokens),
            bytes_accessed=4 * outer * (inner + queries),
            transcendentals=0,
        ),
        name="score",
    )(ids.reshape(tokens, 1), damping, acts, grads, eigenvalues, right, left)


def swap(x, axis):
    return lax.ppermute(x, axis, [(0, 1), (1, 0)])


def place(blocks, at, count):
    rows = blocks[0].shape[0]
    out = jnp.zeros((rows * count,) + blocks[0].shape[1:], blocks[0].dtype)
    for block, index in zip(blocks, at):
        out = lax.dynamic_update_slice_in_dim(out, block, index * rows, 0)
    return out


def gather_line(x, axis, size):
    me = lax.axis_index(axis)
    blocks, at = [x], [me]
    for shift in range(1, size):
        blocks.append(lax.ppermute(x, axis, [(i, (i + shift) % size) for i in range(size)]))
        at.append(lax.rem(me + size - shift, size))
    return blocks, at


def my_half(x, index, own):
    rows = x.shape[0] // 2
    first, second = x[:rows], x[rows:]
    pick_second = (index == 1) if own else (index == 0)
    return jnp.where(pick_second, second, first)


def join(mine, other, index):
    return jnp.where(index == 0, jnp.concatenate([mine, other]), jnp.concatenate([other, mine]))


def flip(x, axis, size, bit):
    return lax.ppermute(x, axis, [(i, i ^ bit) for i in range(size)])


def sum_line(x, axis, size):
    me = lax.axis_index(axis)
    bits, bit = [], 1
    while bit < size:
        index = lax.rem(me // bit, 2)
        x = my_half(x, index, True) + flip(my_half(x, index, False), axis, size, bit)
        bits.append((bit, index))
        bit *= 2
    for bit, index in reversed(bits):
        x = join(x, flip(x, axis, size, bit), index)
    return x


def scatter_sum(x, axes, sizes):
    for axis, size in zip(axes, sizes):
        me = lax.axis_index(axis)
        bit = size // 2
        while bit:
            upper = lax.rem(me // bit, 2) == 1
            wide = x.shape[1] // 2
            first, second = x[:, :wide], x[:, wide:]
            x = jnp.where(upper, second, first) + flip(jnp.where(upper, first, second), axis, size, bit)
            bit //= 2
    return x


def on_device(
    sizes,
    grad_factors,
    act_factors,
    seq_ids,
    out_basis,
    in_basis,
    eigenvalues,
    damping,
    query_out,
    query_in,
    query_ids,
):
    groups, factor, dp, core = sizes
    small = groups == 2 and factor == 4 and dp == 2 and core == 2
    parts = 2 if small else 1
    flat_out = query_out.reshape(-1, query_out.shape[2])
    flat_in = query_in.reshape(-1, query_in.shape[2])
    if small:
        g = lax.axis_index("groups")
        x = lax.axis_index("dp")
        c = lax.axis_index("query")
        pair = join(act_factors, swap(act_factors, "query"), c)
        acts_all = join(pair, swap(pair, "dp"), x)
        grads_all = place(*gather_line(grad_factors, "factor", factor), factor)
        half_in, at = gather_line(my_half(flat_in, g, True), "factor", factor)
        blocks = [flat_in] + [join(b, swap(b, "groups"), g) for b in half_in[1:]]
        right = place(blocks, at, factor)
        half_out = swap(my_half(flat_out, g, True), "dp")
        other_chip = join(half_out, swap(half_out, "groups"), g)
        own_core = join(flat_out, other_chip, x)
        other_core = swap(own_core, "query")
        rows = flat_out.shape[0]
        low = jnp.where(c == 0, own_core, other_core)
        high = jnp.where(c == 0, other_core, own_core)
        left = jnp.concatenate([low[:rows], high[:rows], low[rows:], high[rows:]])
    else:
        acts_all = lax.all_gather(act_factors, ("dp", "query"), axis=0, tiled=True)
        grads_all = lax.all_gather(grad_factors, "factor", axis=0, tiled=True)
        right = lax.all_gather(flat_in, "factor", axis=0, tiled=True)
        left = lax.all_gather(flat_out, ("dp", "query"), axis=0, tiled=True)

    rot_act = rotate(acts_all, in_basis, 0, 1)
    rot_act = sum_line(rot_act, "factor", factor) if small else lax.psum(rot_act, "factor")

    total = None
    for part in range(parts):
        rot_grad = rotate(grads_all, out_basis, part, parts)
        if small:
            mine = my_half(rot_grad, c, True) + swap(my_half(rot_grad, c, False), "query")
            mine = mine + swap(mine, "dp")
            rot_grad = join(mine, swap(mine, "query"), c)
        else:
            rot_grad = lax.psum(rot_grad, ("dp", "query"))
        one = score(seq_ids, damping, rot_act, rot_grad, eigenvalues, right, left, part, parts)
        total = one if total is None else total + one

    count = query_ids.shape[0]
    raw = jnp.sum(total.reshape(SEQS, 8, count, -1), axis=(1, 3))
    raw = raw[:, query_ids]
    return scatter_sum(raw, ("factor", "dp", "query"), (factor, dp, core))


def solution(mesh):
    sizes = tuple(mesh.shape[a] for a in ("groups", "factor", "dp", "query"))
    placed = (
        P(("groups", "factor"), ("dp", "query")),
        P(("groups", "dp", "query"), "factor"),
        P("groups"),
        P(("dp", "query"), "factor"),
        P("factor", ("dp", "query")),
        P("factor", ("dp", "query")),
        P(),
        P(("dp", "query"), None, "factor"),
        P("factor", None, ("dp", "query")),
        P(),
    )
    return jax.shard_map(
        functools.partial(on_device, sizes),
        mesh=mesh,
        in_specs=placed,
        out_specs=P("groups", ("factor", "dp", "query")),
        check_vma=False,
    )
```

```python
import functools

import jax
import jax.numpy as jnp
from jax import lax
from jax.experimental import pallas as pl
from jax.experimental.pallas import tpu as pltpu
from jax.sharding import PartitionSpec as P

SEQS = 4
F32 = jnp.float32
BF16 = jnp.bfloat16
VMEM_BYTES = 56 * 1024 * 1024


def tile_of(width, most):
    for tile in range(most, 0, -128):
        if width % tile == 0:
            return tile
    return width


def halves(x):
    high = x.astype(BF16)
    return high, (x - high.astype(F32)).astype(BF16)


def dot(a, b, contract=((1,), (0,))):
    return lax.dot_general(a, b, (contract, ((), ())), preferred_element_type=F32)


def rotate_kernel(x_ref, basis_ref, out_ref, x_both):
    rows = x_ref.shape[0]

    @pl.when(pl.program_id(0) == 0)
    def _():
        high, low = halves(x_ref[...])
        x_both[:rows, :] = high
        x_both[rows:, :] = low

    high, low = halves(basis_ref[...])
    both = dot(x_both[...], high)
    out_ref[...] = both[:rows] + both[rows:] + dot(x_both[:rows, :], low)


def rotate(x, basis, part, parts):
    rows, depth = x.shape
    width = basis.shape[1] // parts
    tile = tile_of(width, 512)
    steps = width // tile
    return pl.pallas_call(
        rotate_kernel,
        grid=(steps,),
        in_specs=[
            pl.BlockSpec((rows, depth), lambda n: (0, 0)),
            pl.BlockSpec((depth, tile), lambda n: (0, part * steps + n)),
        ],
        out_specs=pl.BlockSpec((rows, tile), lambda n: (0, n)),
        out_shape=jax.ShapeDtypeStruct((rows, width), F32),
        scratch_shapes=[pltpu.VMEM((2 * rows, depth), BF16)],
        compiler_params=pltpu.CompilerParams(vmem_limit_bytes=VMEM_BYTES),
        cost_estimate=pl.CostEstimate(
            flops=6 * rows * depth * width, bytes_accessed=4 * depth * width, transcendentals=0
        ),
        name="rotate",
    )(x, basis)


def score_kernel(ids_ref, damping_ref, acts_ref, grads_ref, eig_ref, right_ref, left_ref, left_ref_2, out_ref, chosen, weighted, right_high, right_low):
    tokens, inner = acts_ref.shape
    span = tokens // 2

    @pl.when(pl.program_id(0) == 0)
    def _():
        out_ref[...] = jnp.zeros_like(out_ref)
        ids = ids_ref[...]
        acts_high, acts_low = halves(acts_ref[...])
        place_in = lax.broadcasted_iota(jnp.int32, (span, tokens), 0)
        token = lax.broadcasted_iota(jnp.int32, (span, tokens), 1)
        for s in range(SEQS):
            start = jnp.sum((ids < s).astype(jnp.int32), axis=1, keepdims=True)
            pick = jnp.where((ids == s) & (token - start == place_in), 1.0, 0.0).astype(BF16)
            chosen[s * span : (s + 1) * span, :] = pick
            high = dot(pick, acts_high).astype(BF16)
            cols = slice(s * inner, (s + 1) * inner)
            weighted[:span, cols] = high
            weighted[span : 2 * span, cols] = dot(pick, acts_low).astype(BF16)
            weighted[2 * span :, cols] = high
        high, low = halves(right_ref[...].T)
        right_high[...] = high
        right_low[...] = low

    rows = eig_ref.shape[0]
    inverse = 1.0 / (eig_ref[...] + damping_ref[0])
    grad_high, grad_low = halves(grads_ref[...])
    grad_high = dot(chosen[...], grad_high).astype(BF16)
    grad_low = dot(chosen[...], grad_low).astype(BF16)
    left = jnp.concatenate([left_ref[...].T, left_ref_2[...].T], axis=1)
    for s in range(SEQS):
        own = slice(s * span, (s + 1) * span)
        grad_all = jnp.concatenate([grad_high[own], grad_high[own], grad_low[own]], axis=0)
        grad_seq = dot(grad_all, weighted[:, s * inner : (s + 1) * inner], ((0,), (0,)))
        high, low = halves(grad_seq * inverse)
        cross = dot(high, right_high[...]) + dot(high, right_low[...]) + dot(low, right_high[...])
        terms = (cross * left).reshape(rows // 8, 8, cross.shape[1])
        out_ref[s * 8 : (s + 1) * 8, :] += jnp.sum(terms, axis=0)


def score(ids, damping, acts, grads, eigenvalues, right, lefts):
    tokens, inner = acts.shape
    queries = right.shape[0]
    outer = eigenvalues.shape[0]
    tile = tile_of(outer, 512)
    steps = outer // tile
    whole = lambda i: (0, 0)
    return pl.pallas_call(
        score_kernel,
        grid=(steps,),
        in_specs=[
            pl.BlockSpec((1, tokens), whole),
            pl.BlockSpec(memory_space=pltpu.SMEM),
            pl.BlockSpec((tokens, inner), whole),
            pl.BlockSpec((tokens, tile), lambda i: (0, i)),
            pl.BlockSpec((tile, inner), lambda i: (i, 0)),
            pl.BlockSpec((queries, inner), whole),
            pl.BlockSpec((queries // 2, tile), lambda i: (0, i)),
            pl.BlockSpec((queries // 2, tile), lambda i: (0, i)),
        ],
        out_specs=pl.BlockSpec((SEQS * 8, queries), whole),
        out_shape=jax.ShapeDtypeStruct((SEQS * 8, queries), F32),
        scratch_shapes=[
            pltpu.VMEM((SEQS * (tokens // 2), tokens), BF16),
            pltpu.VMEM((3 * (tokens // 2), SEQS * inner), BF16),
            pltpu.VMEM((inner, queries), BF16),
            pltpu.VMEM((inner, queries), BF16),
        ],
        compiler_params=pltpu.CompilerParams(vmem_limit_bytes=VMEM_BYTES),
        cost_estimate=pl.CostEstimate(
            flops=6 * SEQS * outer * inner * (queries + 2 * tokens),
            bytes_accessed=4 * outer * (inner + queries),
            transcendentals=0,
        ),
        name="score",
    )(ids.reshape(1, tokens), damping, acts, grads, eigenvalues, right, *lefts)


def swap(x, axis):
    return lax.ppermute(x, axis, [(0, 1), (1, 0)])


def place(blocks, at, count):
    rows = blocks[0].shape[0]
    out = jnp.zeros((rows * count,) + blocks[0].shape[1:], blocks[0].dtype)
    for block, index in zip(blocks, at):
        out = lax.dynamic_update_slice_in_dim(out, block, index * rows, 0)
    return out


def gather_line(x, axis, size):
    me = lax.axis_index(axis)
    blocks, at = [x], [me]
    for shift in range(1, size):
        blocks.append(lax.ppermute(x, axis, [(i, (i + shift) % size) for i in range(size)]))
        at.append(lax.rem(me + size - shift, size))
    return blocks, at


def my_half(x, index, own):
    rows = x.shape[0] // 2
    first, second = x[:rows], x[rows:]
    pick_second = (index == 1) if own else (index == 0)
    return jnp.where(pick_second, second, first)


def join(mine, other, index):
    return jnp.where(index == 0, jnp.concatenate([mine, other]), jnp.concatenate([other, mine]))


def flip(x, axis, size, bit):
    return lax.ppermute(x, axis, [(i, i ^ bit) for i in range(size)])


def sum_line(x, axis, size):
    me = lax.axis_index(axis)
    bits, bit = [], 1
    while bit < size:
        index = lax.rem(me // bit, 2)
        x = my_half(x, index, True) + flip(my_half(x, index, False), axis, size, bit)
        bits.append((bit, index))
        bit *= 2
    for bit, index in reversed(bits):
        x = join(x, flip(x, axis, size, bit), index)
    return x


def scatter_sum(x, axes, sizes):
    for axis, size in zip(axes, sizes):
        me = lax.axis_index(axis)
        bit = size // 2
        while bit:
            upper = lax.rem(me // bit, 2) == 1
            wide = x.shape[1] // 2
            first, second = x[:, :wide], x[:, wide:]
            x = jnp.where(upper, second, first) + flip(jnp.where(upper, first, second), axis, size, bit)
            bit //= 2
    return x


def on_device(
    sizes,
    grad_factors,
    act_factors,
    seq_ids,
    out_basis,
    in_basis,
    eigenvalues,
    damping,
    query_out,
    query_in,
    query_ids,
):
    groups, factor, dp, core = sizes
    small = groups == 2 and factor == 4 and dp == 2 and core == 2
    flat_out = query_out.reshape(-1, query_out.shape[2])
    flat_in = query_in.reshape(-1, query_in.shape[2])
    if small:
        g = lax.axis_index("groups")
        x = lax.axis_index("dp")
        c = lax.axis_index("query")
        tie = lax.optimization_barrier
        pair = join(act_factors, swap(act_factors, "query"), c)
        acts_all = join(pair, swap(pair, "dp"), x)
        grads_all = place(*gather_line(grad_factors, "factor", factor), factor)
        half_out = swap(my_half(flat_out, g, True), "dp")
        acts_all, grads_all, flat_in, half_out = tie((acts_all, grads_all, flat_in, half_out))
        act_part = rotate(acts_all, in_basis, 0, 1)
        half_in, _ = gather_line(my_half(flat_in, g, True), "factor", factor)
        half_out_2 = swap(half_out, "groups")
        act_part, grads_all = tie((act_part, grads_all))
        first = rotate(grads_all, out_basis, 0, 2)
        first, grads_all, half_out_2, half_in = tie((first, grads_all, half_out_2, half_in))
        sent = jnp.concatenate(half_in[1:])
        got = swap(sent, "groups")
        own_core = join(flat_out, join(half_out, half_out_2, g), x)
        other_core = swap(own_core, "query")
        second = rotate(grads_all, out_basis, 1, 2)
        second, got, other_core = tie((second, got, other_core))
        rot_act = sum_line(act_part, "factor", factor)
        rot_grad = jnp.concatenate([first, second], axis=1)
        mine = my_half(rot_grad, c, True) + swap(my_half(rot_grad, c, False), "query")
        mine = mine + swap(mine, "dp")
        rot_grad = join(mine, swap(mine, "query"), c)
        rows = half_in[0].shape[0]
        pieces = [(sent[k * rows : (k + 1) * rows], got[k * rows : (k + 1) * rows]) for k in range(factor - 1)]
        blocks = [flat_in] + [join(b, o, g) for b, o in pieces]
        me = lax.axis_index("factor")
        at = []
        for shift in range(factor):
            owner = lax.rem(me + factor - shift, factor)
            at.append(jnp.where(lax.rem(owner, 2) == c, owner // 2, 2 + owner // 2))
        right = place(blocks, at, factor)
        lefts = (own_core, other_core)
    else:
        acts_all = lax.all_gather(act_factors, ("dp", "query"), axis=0, tiled=True)
        grads_all = lax.all_gather(grad_factors, "factor", axis=0, tiled=True)
        right = lax.all_gather(flat_in, "factor", axis=0, tiled=True)
        left = lax.all_gather(flat_out, ("dp", "query"), axis=0, tiled=True)
        lefts = (left[: left.shape[0] // 2], left[left.shape[0] // 2 :])
        rot_act = lax.psum(rotate(acts_all, in_basis, 0, 1), "factor")
        rot_grad = lax.psum(rotate(grads_all, out_basis, 0, 1), ("dp", "query"))

    total = score(seq_ids, damping, rot_act, rot_grad, eigenvalues, right, lefts)
    count = query_ids.shape[0]
    raw = jnp.sum(total.reshape(SEQS, 8, count, -1), axis=(1, 3))
    if small:
        b = jnp.split(raw, 4, axis=1)
        raw = jnp.where(
            c == 0,
            jnp.concatenate([b[0], b[2], b[1], b[3]], axis=1),
            jnp.concatenate([b[2], b[0], b[3], b[1]], axis=1),
        )
    raw = raw[:, query_ids]
    return scatter_sum(raw, ("factor", "dp", "query"), (factor, dp, core))


def solution(mesh):
    sizes = tuple(mesh.shape[a] for a in ("groups", "factor", "dp", "query"))
    placed = (
        P(("groups", "factor"), ("dp", "query")),
        P(("groups", "dp", "query"), "factor"),
        P("groups"),
        P(("dp", "query"), "factor"),
        P("factor", ("dp", "query")),
        P("factor", ("dp", "query")),
        P(),
        P(("dp", "query"), None, "factor"),
        P("factor", None, ("dp", "query")),
        P(),
    )
    return jax.shard_map(
        functools.partial(on_device, sizes),
        mesh=mesh,
        in_specs=placed,
        out_specs=P("groups", ("factor", "dp", "query")),
        check_vma=False,
    )
```
